768 devices in a mesh: curve: 96 (over z, y), near: 8 (over x, core).
Axes of the slice: x: 4, y: 8, z: 12, core: 2. Of those that a mesh axis runs over, the one named last changes fastest.
Arguments:
- moments: float32 [84, 98304], P(None, ('curve', 'near')), may hold values from -6 to 6
- leaf_source: int32 [189, 98304], P(None, ('curve', 'near')), may hold values from 0 to 383, as said below
- leaf_mask: int32 [189, 98304], P(None, ('curve', 'near')), may hold values 0 or 1
- coarse_source: int32 [189, 1536], P(None, ('curve', 'near')), may hold values from 0 to 5, as said below
- up_shift: float32 [84, 84, 8], replicated, may hold values from -0.25 to 0.25
- down_shift: float32 [84, 84, 8], replicated, may hold values from -0.625 to 0.625
- far_shift: float32 [84, 84, 189], replicated, may hold values from -0.046875 to 0.046875
Outputs:
- field_local: float32 [84, 98304], P(None, ('curve', 'near'))
The draws below stay inside these ranges and needn't reach their ends.
Inputs may be any that keep to these rules, and one draw needn't show every extreme that they name: `leaf_source`: every source is a leaf of the cell's own block of 128 leaves or of the block just before or after it along the curve, never outside the 98304 leaves: leaves of the first block use values of 128 or more, leaves of the last block values under 2 * 128. `coarse_source`: every source is a coarse cell of the cell's own block of 2 coarse cells or of the block just before or after it along the curve, never outside the 1536 cells: cells of the first block use values of 2 or more, cells of the last block values under 2 * 2.
All inputs are finite; a program needn't handle non-finite values. No bound on the sum of `leaf_mask` on one device may be relied on, other than what follows from the above.
Results may differ from the reference program's by a relative error of at most 0.000058.
Values sent between devices are 32-bit elements; how exact they have to be, the bound alone decides.
A program may use at most 64 MiB of HBM per device.

```python
import jax
import jax.numpy as jnp
from jax import lax

P_SIZE = 84
K = 189
LEAF_DEV = 128
LEAVES = 98304
COARSE_DEV = 2
COARSE = 1536


def draw_leaf_source(key, part):
    key = jax.random.fold_in(key, 11)
    position = jnp.arange(LEAVES, dtype=jnp.int32)
    block = position // LEAF_DEV
    last = LEAVES // LEAF_DEV - 1
    lower = jnp.where(block == 0, LEAF_DEV, 0).astype(jnp.int32)
    upper = jnp.where(block == last, 2 * LEAF_DEV, 3 * LEAF_DEV).astype(jnp.int32)
    return jax.random.randint(key, (K, LEAVES), lower[None, :], upper[None, :], dtype=jnp.int32)


def draw_coarse_source(key, part):
    key = jax.random.fold_in(key, 23)
    position = jnp.arange(COARSE, dtype=jnp.int32)
    block = position // COARSE_DEV
    last = COARSE // COARSE_DEV - 1
    lower = jnp.where(block == 0, COARSE_DEV, 0).astype(jnp.int32)
    upper = jnp.where(block == last, 2 * COARSE_DEV, 3 * COARSE_DEV).astype(jnp.int32)
    return jax.random.randint(key, (K, COARSE), lower[None, :], upper[None, :], dtype=jnp.int32)


def place_ends(entries, stream_key, low, largest):
    place = [jax.random.randint(jax.random.fold_in(stream_key, axis), (), 0, length) for axis, length in enumerate(entries.shape)]
    longest = entries.shape.index(max(entries.shape))
    beside = place[:longest] + [(place[longest] + 1) % entries.shape[longest]] + place[longest + 1:]
    return entries.at[tuple(place)].set(low).at[tuple(beside)].set(largest)


def steps_of(own_key, shape, pieces, least, high):
    gain, own = 1.0, jax.random.fold_in(own_key, 6)
    for dim, blocks in pieces:
        heights = jnp.exp(jax.random.uniform(jax.random.fold_in(own, dim), (blocks,), jnp.float32, least / len(pieces), high / len(pieces)))
        gain = gain * jnp.repeat(heights, shape[dim] // blocks).reshape([-1 if axis == dim else 1 for axis in range(len(shape))])
    return gain


def noise(own_key, dims, scale, limit, shards=(), held_as=jnp.bfloat16):
    values = scale * jax.random.normal(own_key, dims, jnp.float32)
    if shards:
        values = values * steps_of(own_key, dims, shards, -0.22, 0.18)
    return jnp.clip(values, -limit, limit).astype(held_as)


def setup_inputs(seed: int = 0) -> dict:
    streams_of = jax.random.split(jax.random.key(seed), 8)
    moments = noise(streams_of[0], (P_SIZE, LEAVES), 1.0, 6.0, ((1, 768),), jnp.float32)
    leaf_source = draw_leaf_source(jax.random.fold_in(streams_of[7], 71), 0)
    leaf_mask = place_ends((jax.random.randint(streams_of[2], (K, LEAVES), 0, 4) < 3).astype(jnp.int32), jax.random.fold_in(streams_of[2], 1), 0, 1)
    coarse_source = draw_coarse_source(jax.random.fold_in(streams_of[7], 71), 0)
    up_shift = noise(streams_of[4], (P_SIZE, P_SIZE, 8), (8 * P_SIZE) ** -0.5, 0.25, (), jnp.float32)
    down_shift = noise(streams_of[5], (P_SIZE, P_SIZE, 8), P_SIZE ** -0.5, 0.625, (), jnp.float32)
    far_shift = noise(streams_of[6], (P_SIZE, P_SIZE, K), (P_SIZE * K) ** -0.5, 0.046875, (), jnp.float32)
    return dict(moments=moments, leaf_source=leaf_source, leaf_mask=leaf_mask, coarse_source=coarse_source, up_shift=up_shift, down_shift=down_shift, far_shift=far_shift)


HIGH = lax.Precision.HIGHEST


def upward(child, up_shift):
    rows = child.shape[0]
    grouped = child.reshape(rows, child.shape[1] // 8, 8)
    return jnp.einsum("pqo,qno->pn", up_shift, grouped, precision=HIGH)


def downward(parent, down_shift):
    rows = parent.shape[0]
    spread = jnp.einsum("pqo,qn->pno", down_shift, parent, precision=HIGH)
    return spread.reshape(rows, parent.shape[1] * 8)


def translate(columns, far_shift):
    rows = far_shift.shape[0]
    flat = far_shift.reshape(rows, rows * far_shift.shape[2])
    return jnp.dot(flat, columns.reshape(rows * far_shift.shape[2], columns.shape[2]), precision=HIGH)


def reference(moments, leaf_source, leaf_mask, coarse_source, up_shift, down_shift, far_shift):
    blocks = LEAVES // LEAF_DEV
    padded = jnp.pad(moments, ((0, 0), (LEAF_DEV, LEAF_DEV)))
    source_blocks = leaf_source.reshape(K, blocks, LEAF_DEV).transpose(1, 0, 2)
    mask_blocks = leaf_mask.reshape(K, blocks, LEAF_DEV).transpose(1, 0, 2)

    def one_block(items):
        number, source, mask = items
        window = lax.dynamic_slice_in_dim(padded, number * LEAF_DEV, 3 * LEAF_DEV, 1)
        columns = jnp.take(window, source, axis=1) * mask.astype(jnp.float32)[None]
        return translate(columns, far_shift)

    far_blocks = lax.map(one_block, (jnp.arange(blocks, dtype=jnp.int32), source_blocks, mask_blocks))
    leaf_far = far_blocks.transpose(1, 0, 2).reshape(P_SIZE, LEAVES)
    coarse_moments = upward(upward(moments, up_shift), up_shift)
    cell_block = (jnp.arange(COARSE, dtype=jnp.int32) // COARSE_DEV).astype(jnp.int32)
    global_source = ((cell_block[None, :] - 1) * COARSE_DEV + coarse_source).astype(jnp.int32)
    coarse_columns = jnp.take(coarse_moments, global_source, axis=1)
    coarse_local = translate(coarse_columns, far_shift)
    mid_local = downward(coarse_local, down_shift)
    return leaf_far + downward(mid_local, down_shift)
```

```python
import jax, jax.numpy as jnp
from jax import lax
from jax.experimental import pallas as pl
from jax.sharding import PartitionSpec
from jax.experimental.pallas import tpu as pltpu
BF, F32 = jnp.bfloat16, jnp.float32
HIGH = lax.Precision.HIGHEST
MESH = pl.DeviceIdType.MESH
P, K, C = 84, 189, 128
G = 7
NG = P // G

def split(v):
    hi = v.astype(BF)
    return hi, (v - hi.astype(F32)).astype(BF)

def tail(v):
    return jnp.concatenate([v, jnp.zeros((v.shape[0], 2 * 128 - K), v.dtype)], axis=1)

def kernel(m_hbm, src_hbm, msk_hbm, cs_hbm, up_hbm, dn_hbm, far_hbm, out_ref,
           win, cwin, src, msk, cs, up, dn, f32, fc, x0, x1, z, acc,
           sem, fsem, send, recv):
    nc, nn = lax.axis_size("curve"), lax.axis_size("near")
    n = nc * nn
    me = lax.axis_index("curve") * nn + lax.axis_index("near")
    def at(i):
        i = lax.rem(i + n, n)
        return (i // nn, lax.rem(i, nn))
    left, right = at(me - 1), at(me + 1)
    bar = pltpu.get_barrier_semaphore()
    for d in (left, right):
        pl.semaphore_signal(bar, inc=1, device_id=d, device_id_type=MESH)
    own = pltpu.make_async_copy(m_hbm, win.at[1], sem.at[0])
    own.start()
    upc = pltpu.make_async_copy(up_hbm, up, sem.at[1]); upc.start()
    src[184:192, :] = jnp.zeros((8, C), jnp.int32)
    msk[184:192, :] = jnp.zeros((8, C), jnp.int32)
    small = [pltpu.make_async_copy(src_hbm, src.at[0:K], sem.at[2]), pltpu.make_async_copy(msk_hbm, msk.at[0:K], sem.at[3]),
             pltpu.make_async_copy(cs_hbm, cs, sem.at[4]), pltpu.make_async_copy(dn_hbm, dn, sem.at[5])]
    def fcopy(q):
        return pltpu.make_async_copy(far_hbm.at[:, q, :], f32.at[q], fsem.at[q])
    def fstart(q, c):
        fcopy(q).start()
        return c
    lax.fori_loop(0, P, fstart, 0)
    for s in small: s.start()
    lane = lax.broadcasted_iota(jnp.int32, (P, C), 1)
    def pick(which):
        y = jnp.zeros((P, C), F32)
        for o in range(8):
            y = jnp.where(which == o, z[pl.ds(o, P, stride=8), :], y)
        return y
    def apply(op, x):
        z[...] = jnp.dot(op[...].reshape(8 * P, P), x, precision=HIGH, preferred_element_type=F32)
    own.wait(); upc.wait()
    apply(up, win[1])
    y = pick(lane % 8)
    for s in (1, 2, 4):
        y = y + pltpu.roll(y, C - s, 1)
    apply(up, y)
    y = pick(jnp.where(lane % 8 == 0, (lane // 8) % 8, -1))
    for s in (8, 16, 32):
        y = y + pltpu.roll(y, C - s, 1)
    cwin[1] = y
    pl.semaphore_wait(bar, 2)
    copies = []
    for j, buf in enumerate((win, cwin)):
        for i, (slot, d) in enumerate(((2, left), (0, right))):
            c = pltpu.make_async_remote_copy(src_ref=buf.at[1], dst_ref=buf.at[slot], send_sem=send.at[2*j+i], recv_sem=recv.at[2*j+i], device_id=d, device_id_type=MESH)
            c.start()
            copies.append(c)
    x1[...] = jnp.zeros_like(x1)
    x0[:, 192:256, :] = jnp.zeros((G, 64, 256), BF)
    lb = lax.broadcasted_iota(jnp.int32, (P, 128), 1) < K - 128
    def fsplit(q, c):
        fcopy(q).wait()
        a = f32[q, :, 0:128]
        b = tail(f32[q, :, 128:K])
        for t, v in enumerate((a, b)):
            hi, lo = split(v)
            l = pl.ds(pl.multiple_of(q * 256 + t * 128, 128), 128)
            fc[0, 0:P, l] = hi
            fc[1, 0:P, l] = lo
        return c
    lax.fori_loop(0, P, fsplit, 0, unroll=2)
    acc[...] = jnp.zeros_like(acc)
    for s in small: s.wait()
    for c in copies: c.wait()
    def gather(g, x):
        for t in range(12):
            r = slice(16 * t, 16 * t + 16)
            s, m = src[r, :], msk[r, :]
            idx = jnp.bitwise_and(s, 127)
            live = m > 0
            ms = ((s < 128) & live, (s >= 128) & (s < 256) & live, (s >= 256) & live)
            for j in range(G):
                v = jnp.zeros((16, C), F32)
                for b in range(3):
                    w = jnp.broadcast_to(win[b, pl.ds(g * G + j, 1), :], (16, C))
                    v = jnp.where(ms[b], jnp.take_along_axis(w, idx, axis=1, mode="promise_in_bounds"), v)
                x[j, r, 0:C], x[j, r, C:2*C] = split(v)
    def product(g, x):
        l = pl.ds(pl.multiple_of(g * (G * 256), 128), G * 256)
        acc[...] += jnp.dot(fc[:, :, l].reshape(192, G * 256), x[...].reshape(G * 256, 256), preferred_element_type=F32)
    def body(i, c):
        product(jnp.maximum(2 * i - 1, 0), x1)
        gather(2 * i, x0)
        product(2 * i, x0)
        gather(2 * i + 1, x1)
        return c
    lax.fori_loop(0, NG // 2, body, 0)
    product(NG - 1, x1)
    total = acc[0:P, 0:C] + (acc[0:P, C:2*C] + (acc[96:96+P, 0:C] + acc[96:96+P, C:2*C]))
    w = jnp.where(lane % 64 == 0, cwin[0], jnp.where(lane % 64 == 1, pltpu.roll(cwin[1], 1, 1), pltpu.roll(cwin[2], 2, 1)))
    for m in range(2):
        for t in range(2):
            s = tail(cs[m:m+1, 128:K]) if t else cs[m:m+1, 0:128]
            idx = jnp.bitwise_and((s & 1) * 64 + (s >> 1), 127)
            xc = jnp.take_along_axis(w, jnp.broadcast_to(idx, (P, C)), axis=1, mode="promise_in_bounds")
            if t:
                xc = jnp.where(lb, xc, 0.0)
            z[(2*m+t)*P:(2*m+t+1)*P, :] = xc
    def cstep(q, a):
        fa, fb = f32[q, :, 0:128], tail(f32[q, :, 128:K])
        return tuple(a[m] + fa * z[pl.ds(2*m*P + q, 1), :] + fb * z[pl.ds((2*m+1)*P + q, 1), :] for m in range(2))
    zero = jnp.zeros((P, C), F32)
    a = lax.fori_loop(0, P, cstep, (zero, zero), unroll=4)
    cl = jnp.where(lane < 64, jnp.sum(a[0], axis=1, keepdims=True), jnp.sum(a[1], axis=1, keepdims=True))
    apply(dn, cl)
    mid = pick((lane // 8) % 8)
    apply(dn, mid)
    total = total + pick(lane % 8)
    out_ref[...] = total

def run(moments, leaf_source, leaf_mask, coarse_source, up_shift, down_shift, far_shift):
    anyspec = pl.BlockSpec(memory_space=pl.ANY)
    V = pltpu.VMEM
    return pl.pallas_call(
        kernel,
        out_shape=jax.ShapeDtypeStruct((P, C), F32),
        in_specs=[anyspec] * 7,
        out_specs=pl.BlockSpec(memory_space=pltpu.VMEM),
        scratch_shapes=[
            V((3, P, C), F32), V((3, P, C), F32), V((192, C), jnp.int32), V((192, C), jnp.int32), V((2, K), jnp.int32),
            V((P, 8, P), F32), V((P, 8, P), F32), V((P, P, K), F32), V((2, 96, P * 256), BF), V((G, 256, 256), BF), V((G, 256, 256), BF),
            V((8 * P, C), F32), V((192, 256), F32),
            pltpu.SemaphoreType.DMA((6,)), pltpu.SemaphoreType.DMA((P,)), pltpu.SemaphoreType.DMA((4,)), pltpu.SemaphoreType.DMA((4,)),
        ],
        compiler_params=pltpu.CompilerParams(vmem_limit_bytes=56 << 20, collective_id=0, has_side_effects=True),
    )(moments, leaf_source, leaf_mask, coarse_source.T, jnp.transpose(up_shift, (0, 2, 1)), jnp.transpose(down_shift, (0, 2, 1)), far_shift)


def solution(mesh):
    cells = PartitionSpec(None, ("curve", "near"))
    copied = PartitionSpec()
    return jax.shard_map(run, mesh=mesh, in_specs=(cells,) * 4 + (copied,) * 3, out_specs=cells, check_vma=False)
```

```python
import jax, jax.numpy as jnp
from jax import lax
from jax.experimental import pallas as pl
from jax.experimental.pallas import tpu as pltpu
from jax.sharding import PartitionSpec
BF, F32, I32 = jnp.bfloat16, jnp.float32, jnp.int32
MESH = pl.DeviceIdType.MESH
P, K, C = 84, 189, 128
LO = 96
FC = 7
FW = 14


def rounded(v):
    return v.astype(BF).astype(F32)


def split(v):
    hi = v.astype(BF)
    return hi, (v - hi.astype(F32)).astype(BF)


def tail(v):
    return jnp.concatenate([v, jnp.zeros((v.shape[0], 2 * 128 - K), v.dtype)], axis=1)


def lanes(rows):
    return lax.broadcasted_iota(I32, (rows, C), 1)


def take(v, index):
    return jnp.take_along_axis(v, index, axis=1, mode="promise_in_bounds")


def kernel(m_hbm, src_hbm, msk_hbm, cs_hbm, up_hbm, dn_hbm, far_hbm, out_ref,
           win, cwin, src, msk, cs, up, dn, u3, d3, rr, z, f32, fw, fc, xp, xx, xc, ca, acc,
           sem, fsem, send, recv):
    nn = lax.axis_size("near")
    n = lax.axis_size("curve") * nn
    me = lax.axis_index("curve") * nn + lax.axis_index("near")
    early = lax.rem(me, 2) == 0
    has = (me > 0, me < n - 1)
    bar = pltpu.get_barrier_semaphore()

    def at(i):
        i = lax.rem(i + n, n)
        return (i // nn, lax.rem(i, nn))

    ends = (at(me - 1), at(me + 1))
    for side in range(2):
        @pl.when(has[side])
        def _():
            pl.semaphore_signal(bar, inc=1, device_id=ends[side], device_id_type=MESH)

    def remote(j, side):
        buf = (win, cwin)[j]
        return pltpu.make_async_remote_copy(
            src_ref=buf.at[1], dst_ref=buf.at[2 - 2 * side], send_sem=send.at[2 * j + side],
            recv_sem=recv.at[2 * j + 1 - side], device_id=ends[side], device_id_type=MESH)

    def each(cond, sides, act):
        for side in sides:
            @pl.when(jnp.logical_and(cond, has[side]))
            def _():
                act(side)

    def meet(cond):
        @pl.when(cond)
        def _():
            pl.semaphore_wait(bar, has[0].astype(I32) + has[1].astype(I32))

    own = pltpu.make_async_copy(m_hbm, win.at[1], sem.at[0])
    upc = pltpu.make_async_copy(up_hbm, up, sem.at[1])
    own.start()
    upc.start()
    src[184:192, :] = jnp.zeros((8, C), I32)
    msk[184:192, :] = jnp.zeros((8, C), I32)
    small = [pltpu.make_async_copy(a, b, sem.at[2 + i]) for i, (a, b) in enumerate(
        ((src_hbm, src.at[0:K]), (msk_hbm, msk.at[0:K]), (cs_hbm, cs), (dn_hbm, dn)))]

    def fcopy(q):
        return pltpu.make_async_copy(far_hbm.at[:, q, :], f32.at[q], fsem.at[lax.div(q, FW)])

    def fstart(q, c):
        fcopy(q).start()
        return c

    lax.fori_loop(0, P, fstart, 0)
    for s in small:
        s.start()
    lane = lanes(P)
    rr[248:256, :] = jnp.zeros((8, C), F32)

    def triple(dst, op):
        v = op[...].reshape(8 * P, P)
        hi = rounded(v)
        dst[...] = jnp.concatenate([hi, hi, v - hi, jnp.zeros((8 * P, 4), F32)], axis=1)

    def apply(op3, x):
        hi = rounded(x)
        rr[0:P, :] = hi
        rr[P:2 * P, :] = x - hi
        rr[2 * P:3 * P, :] = hi
        z[...] = jnp.dot(op3[...], rr[...], preferred_element_type=F32)

    def pick(which):
        y = jnp.zeros((P, C), F32)
        for o in range(8):
            y = jnp.where(which == o, z[pl.ds(o, P, stride=8), :], y)
        return y

    own.wait()
    meet(early)
    each(early, (0, 1), lambda side: remote(0, side).start())
    for side in range(2):
        @pl.when(jnp.logical_not(has[side]))
        def _():
            win[2 * side] = jnp.zeros((P, C), F32)
            cwin[2 * side] = jnp.zeros((P, C), F32)
    upc.wait()
    triple(u3, up)
    apply(u3, win[1])
    y = pick(lane % 8)
    for s in (1, 2, 4):
        y = y + pltpu.roll(y, C - s, 1)
    apply(u3, y)
    y = pick(jnp.where(lane % 8 == 0, (lane // 8) % 8, -1))
    for s in (8, 16, 32):
        y = y + pltpu.roll(y, C - s, 1)
    cwin[1] = y
    each(early, (0, 1), lambda side: remote(1, side).start())
    for s in small:
        s.wait()

    def gather(b, store, part, beside=None):
        def body(t, c):
            r = pl.ds(pl.multiple_of(t * 16, 16), 16)
            s, m = src[r, :], msk[r, :]
            index = jnp.bitwise_and(s, 127)
            hit = jnp.logical_and(lax.shift_right_logical(s, 7) == b, m > 0)
            if beside is not None:
                beside(t)
            for q in range(P):
                v = xp[q, r, :] if part else jnp.zeros((16, C), F32)
                w = jnp.broadcast_to(win[b, pl.ds(q, 1), :], (16, C))
                store(q, r, jnp.where(hit, take(w, index), v))
            return c
        lax.fori_loop(0, 12, body, 0)

    def whole(q, r, v):
        xp[q, r, :] = v

    def halves(q, r, v):
        xx[q, r, 0:C], xx[q, r, C:2 * C] = split(v)

    acc[...] = jnp.zeros_like(acc)
    xx[:, 192:256, :] = jnp.zeros((P, 64, 256), BF)
    triple(d3, dn)

    def fsplit(t):
        @pl.when(lax.rem(t, 2) == 0)
        def _():
            pltpu.make_async_copy(fw, fw, fsem.at[lax.div(t, 2)]).wait()

        for j in range(FC):
            q = t * FC + j
            for i, v in enumerate((f32[q, :, 0:128], tail(f32[q, :, 128:K]))):
                l = pl.ds(pl.multiple_of(q * 256 + i * 128, 128), 128)
                fc[0:P, l], fc[LO:LO + P, l] = split(v)

    gather(1, whole, False, fsplit)
    def coarse_sources():
        w = jnp.where(lane % 64 == 0, cwin[0], jnp.where(lane % 64 == 1, pltpu.roll(cwin[1], 1, 1), pltpu.roll(cwin[2], 2, 1)))
        for m in range(2):
            for t in range(2):
                s = tail(cs[m:m + 1, 128:K]) if t else cs[m:m + 1, 0:128]
                index = jnp.bitwise_and(jnp.bitwise_and(s, 1) * 64 + lax.shift_right_logical(s, 1), 127)
                x = take(w, jnp.broadcast_to(index, (P, C)))
                for q in range(P):
                    xc[2 * m + t, q] = jnp.broadcast_to(x[q:q + 1, :], (8, C))
        ca[...] = jnp.zeros_like(ca)

    def coarse(t):
        for i in range(11):
            r = slice(8 * i, min(8 * i + 8, P))
            n = r.stop - r.start
            sums = [ca[m, r, :] for m in range(2)]
            for j in range(FC):
                q = t * FC + j
                fa, fb = f32[q, r, 0:128], tail(f32[q, r, 128:K])
                for m in range(2):
                    sums[m] = sums[m] + fa * xc[2 * m, q, 0:n, :] + fb * xc[2 * m + 1, q, 0:n, :]
            for m in range(2):
                ca[m, r, :] = sums[m]

    late = jnp.logical_not(early)
    odd_one = me == 1
    send_both = lambda side: (remote(0, side).start(), remote(1, side).start())
    others = jnp.logical_and(late, jnp.logical_not(odd_one))
    meet(others)
    each(others, (0, 1), send_both)
    b1 = jnp.where(odd_one, 2, 0)
    each(odd_one, (1,), lambda side: remote(0, 1 - side).wait_recv())
    each(jnp.logical_not(odd_one), (0,), lambda side: remote(0, 1 - side).wait_recv())
    gather(b1, whole, True)
    meet(odd_one)
    each(odd_one, (0, 1), send_both)
    each(odd_one, (0,), lambda side: remote(0, 1 - side).wait_recv())
    each(jnp.logical_not(odd_one), (1,), lambda side: remote(0, 1 - side).wait_recv())
    each(True, (0, 1), lambda side: remote(1, 1 - side).wait_recv())
    coarse_sources()
    gather(2 - b1, halves, True, coarse)
    acc[...] = jnp.dot(fc[...], xx[...].reshape(P * 256, 256), preferred_element_type=F32)
    cl = jnp.where(lane < 64, *(jnp.sum(ca[m], axis=1, keepdims=True) for m in range(2)))
    apply(d3, cl)
    apply(d3, pick((lane // 8) % 8))
    far = acc[0:P, 0:C] + (acc[0:P, C:2 * C] + (acc[LO:LO + P, 0:C] + acc[LO:LO + P, C:2 * C]))
    out_ref[...] = far + pick(lane % 8)
    each(True, (0, 1), lambda side: (remote(0, side).wait_send(), remote(1, side).wait_send()))


def run(moments, leaf_source, leaf_mask, coarse_source, up_shift, down_shift, far_shift):
    V = pltpu.VMEM
    D = pltpu.SemaphoreType.DMA
    return pl.pallas_call(
        kernel,
        out_shape=jax.ShapeDtypeStruct((P, C), F32),
        in_specs=[pl.BlockSpec(memory_space=pl.ANY)] * 7,
        out_specs=pl.BlockSpec(memory_space=pltpu.VMEM),
        scratch_shapes=[
            V((3, P, C), F32), V((3, P, C), F32), V((192, C), I32), V((192, C), I32), V((2, K), I32),
            V((P, 8, P), F32), V((P, 8, P), F32), V((8 * P, 256), F32), V((8 * P, 256), F32), V((256, C), F32), V((8 * P, C), F32),
            V((P, P, K), F32), V((P * FW // 8, 8, K), F32), V((2 * LO, P * 256), BF), V((P, 192, C), F32), V((P, 256, 256), BF),
            V((4, P, 8, C), F32), V((2, P, C), F32), V((2 * LO, 256), F32),
            D((6,)), D((P // FW,)), D((4,)), D((4,)),
        ],
        compiler_params=pltpu.CompilerParams(vmem_limit_bytes=58 << 20, collective_id=0, has_side_effects=True),
    )(moments, leaf_source, leaf_mask, coarse_source.T, jnp.transpose(up_shift, (0, 2, 1)), jnp.transpose(down_shift, (0, 2, 1)), far_shift)


def solution(mesh):
    cells = PartitionSpec(None, ("curve", "near"))
    copied = PartitionSpec()
    return jax.shard_map(run, mesh=mesh, in_specs=(cells,) * 4 + (copied,) * 3, out_specs=cells, check_vma=False)
```

```python
import jax, jax.numpy as jnp
from jax import lax
from jax.experimental import pallas as pl
from jax.experimental.pallas import tpu as pltpu
from jax.sharding import PartitionSpec
BF, F32, I32 = jnp.bfloat16, jnp.float32, jnp.int32
MESH = pl.DeviceIdType.MESH
P, K, C = 84, 189, 128
LO = 96
FC = 7
FW = 14


def rounded(v):
    return v.astype(BF).astype(F32)


def split(v):
    hi = v.astype(BF)
    return hi, (v - hi.astype(F32)).astype(BF)


def tail(v):
    return jnp.concatenate([v, jnp.zeros((v.shape[0], 2 * 128 - K), v.dtype)], axis=1)


def lanes(rows):
    return lax.broadcasted_iota(I32, (rows, C), 1)


def take(v, index):
    return jnp.take_along_axis(v, index, axis=1, mode="promise_in_bounds")


def kernel(m_hbm, src_hbm, msk_hbm, cs_hbm, up_hbm, dn_hbm, far_hbm, out_ref,
           win, cwin, src, msk, cs, up, dn, u3, d3, rr, z, f32, fw, fa, fb, xp, xa, xb, xc, ca, acc,
           sem, fsem, send, recv):
    nn = lax.axis_size("near")
    n = lax.axis_size("curve") * nn
    me = lax.axis_index("curve") * nn + lax.axis_index("near")
    has = (me > 0, me < n - 1)
    bar = pltpu.get_barrier_semaphore()

    def at(i):
        i = lax.rem(i + n, n)
        return (i // nn, lax.rem(i, nn))

    ends = (at(me - 1), at(me + 1))
    for side in range(2):
        @pl.when(has[side])
        def _():
            pl.semaphore_signal(bar, inc=1, device_id=ends[side], device_id_type=MESH)

    def remote(j, side):
        return pltpu.make_async_remote_copy(
            src_ref=cwin.at[1] if j else m_hbm, dst_ref=(win, cwin)[j].at[2 - 2 * side], send_sem=send.at[2 * j + side],
            recv_sem=recv.at[2 * j + 1 - side], device_id=ends[side], device_id_type=MESH)

    def each(cond, sides, act):
        for side in sides:
            @pl.when(jnp.logical_and(cond, has[side]))
            def _():
                act(side)

    def meet(cond):
        @pl.when(cond)
        def _():
            pl.semaphore_wait(bar, has[0].astype(I32) + has[1].astype(I32))

    own = pltpu.make_async_copy(m_hbm, win.at[1], sem.at[0])
    upc = pltpu.make_async_copy(up_hbm, up, sem.at[1])
    own.start()
    upc.start()
    meet(me == 0)
    each(me == 0, (0, 1), lambda side: remote(0, side).start())
    src[184:192, :] = jnp.zeros((8, C), I32)
    msk[184:192, :] = jnp.zeros((8, C), I32)
    small = [pltpu.make_async_copy(a, b, sem.at[2 + i]) for i, (a, b) in enumerate(
        ((src_hbm, src.at[0:K]), (msk_hbm, msk.at[0:K]), (cs_hbm, cs), (dn_hbm, dn)))]

    def fcopy(q):
        return pltpu.make_async_copy(far_hbm.at[:, q, :], f32.at[q], fsem.at[lax.div(q, FW)])

    def fstart(q, c):
        fcopy(q).start()
        return c

    lax.fori_loop(0, P, fstart, 0)
    for s in small:
        s.start()
    lane = lanes(P)
    rr[248:256, :] = jnp.zeros((8, C), F32)

    def triple(dst, op):
        v = op[...].reshape(8 * P, P)
        hi = rounded(v)
        dst[...] = jnp.concatenate([hi, hi, v - hi, jnp.zeros((8 * P, 4), F32)], axis=1)

    def apply(op3, x):
        hi = rounded(x)
        rr[0:P, :] = hi
        rr[P:2 * P, :] = x - hi
        rr[2 * P:3 * P, :] = hi
        z[...] = jnp.dot(op3[...], rr[...], preferred_element_type=F32)

    def pick(which):
        y = jnp.zeros((P, C), F32)
        for o in range(8):
            y = jnp.where(which == o, z[pl.ds(o, P, stride=8), :], y)
        return y

    own.wait()
    for side in range(2):
        @pl.when(jnp.logical_not(has[side]))
        def _():
            win[2 * side] = jnp.zeros((P, C), F32)
            cwin[2 * side] = jnp.zeros((P, C), F32)
    upc.wait()
    triple(u3, up)
    apply(u3, win[1])
    y = pick(lane % 8)
    for s in (1, 2, 4):
        y = y + pltpu.roll(y, C - s, 1)
    apply(u3, y)
    y = pick(jnp.where(lane % 8 == 0, (lane // 8) % 8, -1))
    for s in (8, 16, 32):
        y = y + pltpu.roll(y, C - s, 1)
    cwin[1] = y
    mid = me > 1
    meet(mid)
    each(mid, (0, 1), lambda side: (remote(0, side).start(), remote(1, side).start()))
    each(me == 0, (0, 1), lambda side: remote(1, side).start())
    for s in small:
        s.wait()

    def gather(b, steps, store, part, beside=None):
        def body(t, c):
            r = pl.ds(pl.multiple_of(t * 16, 16), 16)
            s, m = src[r, :], msk[r, :]
            index = jnp.bitwise_and(s, 127)
            hit = jnp.logical_and(lax.shift_right_logical(s, 7) == b, m > 0)
            if beside is not None:
                beside(t)
            for q in range(P):
                v = xp[q, r, :] if part else jnp.zeros((16, C), F32)
                w = jnp.broadcast_to(win[b, pl.ds(q, 1), :], (16, C))
                store(q, t, r, jnp.where(hit, take(w, index), v))
            return c
        lax.fori_loop(*steps, body, 0)

    def whole(q, t, r, v):
        xp[q, r, :] = v

    def halves_a(q, t, r, v):
        xa[q, r, 0:C], xa[q, r, C:2 * C] = split(v)

    def halves_b(q, t, r, v):
        r = pl.ds(pl.multiple_of((t - 8) * 16, 16), 16)
        xb[q, r, 0:C], xb[q, r, C:2 * C] = split(v)

    acc[...] = jnp.zeros_like(acc)
    xb[:, 64:C, :] = jnp.zeros((P, C - 64, 256), BF)
    triple(d3, dn)

    def fsplit(t):
        @pl.when(lax.rem(t, 2) == 0)
        def _():
            pltpu.make_async_copy(fw, fw, fsem.at[lax.div(t, 2)]).wait()

        for j in range(FC):
            q = t * FC + j
            l = pl.ds(pl.multiple_of(q * C, C), C)
            for f, v in ((fa, f32[q, :, 0:C]), (fb, tail(f32[q, :, C:K]))):
                f[0:P, l], f[LO:LO + P, l] = split(v)

    gather(1, (0, 12), whole, False, fsplit)
    def coarse_sources():
        w = jnp.where(lane % 64 == 0, cwin[0], jnp.where(lane % 64 == 1, pltpu.roll(cwin[1], 1, 1), pltpu.roll(cwin[2], 2, 1)))
        for m in range(2):
            for t in range(2):
                s = tail(cs[m:m + 1, 128:K]) if t else cs[m:m + 1, 0:128]
                index = jnp.bitwise_and(jnp.bitwise_and(s, 1) * 64 + lax.shift_right_logical(s, 1), 127)
                x = take(w, jnp.broadcast_to(index, (P, C)))
                for q in range(P):
                    xc[2 * m + t, q] = jnp.broadcast_to(x[q:q + 1, :], (8, C))
        ca[...] = jnp.zeros_like(ca)

    def beside_b(t):
        t = t - 8
        step = P // 4
        l = pl.ds(pl.multiple_of(t * (step * C), C), step * C)
        acc[...] += jnp.dot(fa[:, l], xa[pl.ds(t * step, step)].reshape(step * C, 2 * C), preferred_element_type=F32)
        for i in range(11):
            r = slice(8 * i, min(8 * i + 8, P))
            n = r.stop - r.start
            sums = [ca[m, r, :] for m in range(2)]
            for j in range(step):
                q = t * step + j
                u, v = f32[q, r, 0:C], tail(f32[q, r, C:K])
                for m in range(2):
                    sums[m] = sums[m] + u * xc[2 * m, q, 0:n, :] + v * xc[2 * m + 1, q, 0:n, :]
            for m in range(2):
                ca[m, r, :] = sums[m]

    one = me == 1
    rest = jnp.logical_not(one)
    b1 = jnp.where(one, 2, 0)
    each(one, (1,), lambda side: remote(0, 1 - side).wait_recv())
    each(rest, (0,), lambda side: remote(0, 1 - side).wait_recv())
    gather(b1, (0, 12), whole, True)
    meet(one)
    each(one, (0, 1), lambda side: (remote(0, side).start(), remote(1, side).start()))
    each(one, (0,), lambda side: remote(0, 1 - side).wait_recv())
    each(rest, (1,), lambda side: remote(0, 1 - side).wait_recv())
    gather(2 - b1, (0, 8), halves_a, True)
    each(True, (0, 1), lambda side: remote(1, 1 - side).wait_recv())
    coarse_sources()
    gather(2 - b1, (8, 12), halves_b, True, beside_b)
    acc[...] += jnp.dot(fb[...], xb[...].reshape(P * C, 2 * C), preferred_element_type=F32)
    cl = jnp.where(lane < 64, *(jnp.sum(ca[m], axis=1, keepdims=True) for m in range(2)))
    apply(d3, cl)
    apply(d3, pick((lane // 8) % 8))
    far = acc[0:P, 0:C] + (acc[0:P, C:2 * C] + (acc[LO:LO + P, 0:C] + acc[LO:LO + P, C:2 * C]))
    out_ref[...] = far + pick(lane % 8)
    each(True, (0, 1), lambda side: (remote(0, side).wait_send(), remote(1, side).wait_send()))


def run(moments, leaf_source, leaf_mask, coarse_source, up_shift, down_shift, far_shift):
    V = pltpu.VMEM
    D = pltpu.SemaphoreType.DMA
    return pl.pallas_call(
        kernel,
        out_shape=jax.ShapeDtypeStruct((P, C), F32),
        in_specs=[pl.BlockSpec(memory_space=pl.ANY)] * 7,
        out_specs=pl.BlockSpec(memory_space=pltpu.VMEM),
        scratch_shapes=[
            V((3, P, C), F32), V((3, P, C), F32), V((192, C), I32), V((192, C), I32), V((2, K), I32),
            V((P, 8, P), F32), V((P, 8, P), F32), V((8 * P, 256), F32), V((8 * P, 256), F32), V((256, C), F32), V((8 * P, C), F32),
            V((P, P, K), F32), V((P * FW // 8, 8, K), F32), V((2 * LO, P * C), BF), V((2 * LO, P * C), BF), V((P, 192, C), F32), V((P, C, 256), BF), V((P, C, 256), BF),
            V((4, P, 8, C), F32), V((2, P, C), F32), V((2 * LO, 256), F32),
            D((6,)), D((P // FW,)), D((4,)), D((4,)),
        ],
        compiler_params=pltpu.CompilerParams(vmem_limit_bytes=58 << 20, collective_id=0, has_side_effects=True),
    )(moments, leaf_source, leaf_mask, coarse_source.T, jnp.transpose(up_shift, (0, 2, 1)), jnp.transpose(down_shift, (0, 2, 1)), far_shift)


def solution(mesh):
    cells = PartitionSpec(None, ("curve", "near"))
    copied = PartitionSpec()
    return jax.shard_map(run, mesh=mesh, in_specs=(cells,) * 4 + (copied,) * 3, out_specs=cells, check_vma=False)
```

```python
import jax, jax.numpy as jnp
from jax import lax
from jax.experimental import pallas as pl
from jax.experimental.pallas import tpu as pltpu
from jax.sharding import PartitionSpec
BF, F32, I32 = jnp.bfloat16, jnp.float32, jnp.int32
MESH = pl.DeviceIdType.MESH
P, K, C = 84, 189, 128
LO = 96
FC = 7
FW = 14


def rounded(v):
    return v.astype(BF).astype(F32)


def split(v):
    hi = v.astype(BF)
    return hi, (v - hi.astype(F32)).astype(BF)


def tail(v):
    return jnp.concatenate([v, jnp.zeros((v.shape[0], 2 * 128 - K), v.dtype)], axis=1)


def lanes(rows):
    return lax.broadcasted_iota(I32, (rows, C), 1)


def take(v, index):
    return jnp.take_along_axis(v, index, axis=1, mode="promise_in_bounds")


def kernel(m_hbm, src_hbm, msk_hbm, cs_hbm, up_hbm, dn_hbm, far_hbm, out_ref,
           win, cwin, src, msk, cs, up, dn, u3, d3, rr, z, f32, fw, fa, fb, xp, xa, xb, xc, ca, acc,
           sem, fsem, send, recv):
    nn = lax.axis_size("near")
    n = lax.axis_size("curve") * nn
    me = lax.axis_index("curve") * nn + lax.axis_index("near")
    has = (me > 0, me < n - 1)
    bar = pltpu.get_barrier_semaphore()

    def at(i):
        i = lax.rem(i + n, n)
        return (i // nn, lax.rem(i, nn))

    ends = (at(me - 1), at(me + 1))
    for side in range(2):
        @pl.when(has[side])
        def _():
            pl.semaphore_signal(bar, inc=1, device_id=ends[side], device_id_type=MESH)

    def remote(j, side):
        return pltpu.make_async_remote_copy(
            src_ref=cwin.at[1] if j else m_hbm, dst_ref=(win, cwin)[j].at[2 - 2 * side], send_sem=send.at[2 * j + side],
            recv_sem=recv.at[2 * j + 1 - side], device_id=ends[side], device_id_type=MESH)

    def each(cond, sides, act):
        for side in sides:
            @pl.when(jnp.logical_and(cond, has[side]))
            def _():
                act(side)

    def meet(cond):
        @pl.when(cond)
        def _():
            pl.semaphore_wait(bar, has[0].astype(I32) + has[1].astype(I32))

    own = pltpu.make_async_copy(m_hbm, win.at[1], sem.at[0])
    upc = pltpu.make_async_copy(up_hbm, up, sem.at[1])
    own.start()
    upc.start()
    meet(me == 0)
    each(me == 0, (0, 1), lambda side: remote(0, side).start())
    src[184:192, :] = jnp.zeros((8, C), I32)
    msk[184:192, :] = jnp.zeros((8, C), I32)
    small = [pltpu.make_async_copy(a, b, sem.at[2 + i]) for i, (a, b) in enumerate(
        ((src_hbm, src.at[0:K]), (msk_hbm, msk.at[0:K]), (cs_hbm, cs), (dn_hbm, dn)))]

    def fcopy(q):
        return pltpu.make_async_copy(far_hbm.at[:, q, :], f32.at[q], fsem.at[lax.div(q, FW)])

    def fstart(q, c):
        fcopy(q).start()
        return c

    lax.fori_loop(0, P, fstart, 0)
    for s in small:
        s.start()
    lane = lanes(P)
    rr[248:256, :] = jnp.zeros((8, C), F32)

    def triple(dst, op):
        v = op[...].reshape(8 * P, P)
        hi = rounded(v)
        dst[...] = jnp.concatenate([hi, hi, v - hi, jnp.zeros((8 * P, 4), F32)], axis=1)

    def apply(op3, x):
        hi = rounded(x)
        rr[0:P, :] = hi
        rr[P:2 * P, :] = x - hi
        rr[2 * P:3 * P, :] = hi
        z[...] = jnp.dot(op3[...], rr[...], preferred_element_type=F32)

    def pick(which):
        y = jnp.zeros((P, C), F32)
        for o in range(8):
            y = jnp.where(which == o, z[pl.ds(o, P, stride=8), :], y)
        return y

    own.wait()
    for side in range(2):
        @pl.when(jnp.logical_not(has[side]))
        def _():
            win[2 * side] = jnp.zeros((P, C), F32)
            cwin[2 * side] = jnp.zeros((P, C), F32)
    upc.wait()
    triple(u3, up)
    apply(u3, win[1])
    y = pick(lane % 8)
    for s in (1, 2, 4):
        y = y + pltpu.roll(y, C - s, 1)
    apply(u3, y)
    y = pick(jnp.where(lane % 8 == 0, (lane // 8) % 8, -1))
    for s in (8, 16, 32):
        y = y + pltpu.roll(y, C - s, 1)
    cwin[1] = y
    mid = me > 1
    meet(mid)
    each(mid, (0, 1), lambda side: (remote(0, side).start(), remote(1, side).start()))
    each(me == 0, (0, 1), lambda side: remote(1, side).start())
    for s in small:
        s.wait()

    def gather(b, steps, store, part, beside=None):
        def body(t, c):
            r = pl.ds(pl.multiple_of(t * 16, 16), 16)
            s, m = src[r, :], msk[r, :]
            index = jnp.bitwise_and(s, 127)
            hit = jnp.logical_and(lax.shift_right_logical(s, 7) == b, m > 0)
            if beside is not None:
                beside(t)
            for q in range(P):
                v = xp[q, r, :] if part else jnp.zeros((16, C), F32)
                w = jnp.broadcast_to(win[b, pl.ds(q, 1), :], (16, C))
                store(q, t, r, jnp.where(hit, take(w, index), v))
            return c
        lax.fori_loop(*steps, body, 0)

    def whole(q, t, r, v):
        xp[q, r, :] = v

    def halves_a(q, t, r, v):
        xa[q, r, 0:C], xa[q, r, C:2 * C] = split(v)

    def halves_b(q, t, r, v):
        r = pl.ds(pl.multiple_of((t - 8) * 16, 16), 16)
        xb[q, r, 0:C], xb[q, r, C:2 * C] = split(v)

    acc[...] = jnp.zeros_like(acc)
    xb[:, 64:C, :] = jnp.zeros((P, C - 64, 256), BF)
    triple(d3, dn)

    def fsplit(t):
        @pl.when(lax.rem(t, 2) == 0)
        def _():
            pltpu.make_async_copy(fw, fw, fsem.at[lax.div(t, 2)]).wait()

        for j in range(FC):
            q = t * FC + j
            l = pl.ds(pl.multiple_of(q * C, C), C)
            for f, v in ((fa, f32[q, :, 0:C]), (fb, tail(f32[q, :, C:K]))):
                f[0:P, l], f[LO:LO + P, l] = split(v)

    gather(1, (0, 12), whole, False, fsplit)
    def coarse_sources():
        w = jnp.where(lane % 64 == 0, cwin[0], jnp.where(lane % 64 == 1, pltpu.roll(cwin[1], 1, 1), pltpu.roll(cwin[2], 2, 1)))
        for m in range(2):
            for t in range(2):
                s = tail(cs[m:m + 1, 128:K]) if t else cs[m:m + 1, 0:128]
                index = jnp.bitwise_and(jnp.bitwise_and(s, 1) * 64 + lax.shift_right_logical(s, 1), 127)
                x = take(w, jnp.broadcast_to(index, (P, C)))
                for q in range(P):
                    xc[2 * m + t, q] = jnp.broadcast_to(x[q:q + 1, :], (8, C))
        ca[...] = jnp.zeros_like(ca)

    def beside_b(t):
        t = t - 8
        step = P // 4
        l = pl.ds(pl.multiple_of(t * (step * C), C), step * C)
        acc[...] += jnp.dot(fa[:, l], xa[pl.ds(t * step, step)].reshape(step * C, 2 * C), preferred_element_type=F32)
        for i in range(11):
            r = slice(8 * i, min(8 * i + 8, P))
            n = r.stop - r.start
            sums = [ca[m, r, :] for m in range(2)]
            for j in range(step):
                q = t * step + j
                u, v = f32[q, r, 0:C], tail(f32[q, r, C:K])
                for m in range(2):
                    sums[m] = sums[m] + u * xc[2 * m, q, 0:n, :] + v * xc[2 * m + 1, q, 0:n, :]
            for m in range(2):
                ca[m, r, :] = sums[m]

    one = me == 1
    near_one = jnp.logical_or(one, me == 2)
    rest = jnp.logical_not(near_one)
    b1 = jnp.where(near_one, 2, 0)
    each(near_one, (1,), lambda side: remote(0, 1 - side).wait_recv())
    each(rest, (0,), lambda side: remote(0, 1 - side).wait_recv())
    gather(b1, (0, 12), whole, True)
    meet(one)
    each(one, (0, 1), lambda side: (remote(0, side).start(), remote(1, side).start()))
    each(near_one, (0,), lambda side: remote(0, 1 - side).wait_recv())
    each(rest, (1,), lambda side: remote(0, 1 - side).wait_recv())
    gather(2 - b1, (0, 8), halves_a, True)
    each(True, (0, 1), lambda side: remote(1, 1 - side).wait_recv())
    coarse_sources()
    gather(2 - b1, (8, 12), halves_b, True, beside_b)
    acc[...] += jnp.dot(fb[...], xb[...].reshape(P * C, 2 * C), preferred_element_type=F32)
    cl = jnp.where(lane < 64, *(jnp.sum(ca[m], axis=1, keepdims=True) for m in range(2)))
    apply(d3, cl)
    apply(d3, pick((lane // 8) % 8))
    far = acc[0:P, 0:C] + (acc[0:P, C:2 * C] + (acc[LO:LO + P, 0:C] + acc[LO:LO + P, C:2 * C]))
    out_ref[...] = far + pick(lane % 8)
    each(True, (0, 1), lambda side: (remote(0, side).wait_send(), remote(1, side).wait_send()))


def run(moments, leaf_source, leaf_mask, coarse_source, up_shift, down_shift, far_shift):
    V = pltpu.VMEM
    D = pltpu.SemaphoreType.DMA
    return pl.pallas_call(
        kernel,
        out_shape=V((P, C), F32),
        in_specs=[pl.BlockSpec(memory_space=pl.ANY)] * 7,
        out_specs=pl.BlockSpec(memory_space=pltpu.VMEM),
        scratch_shapes=[
            V((3, P, C), F32), V((3, P, C), F32), V((192, C), I32), V((192, C), I32), V((2, K), I32),
            V((P, 8, P), F32), V((P, 8, P), F32), V((8 * P, 256), F32), V((8 * P, 256), F32), V((256, C), F32), V((8 * P, C), F32),
            V((P, P, K), F32), V((P * FW // 8, 8, K), F32), V((2 * LO, P * C), BF), V((2 * LO, P * C), BF), V((P, 192, C), F32), V((P, C, 256), BF), V((P, C, 256), BF),
            V((4, P, 8, C), F32), V((2, P, C), F32), V((2 * LO, 256), F32),
            D((6,)), D((P // FW,)), D((4,)), D((4,)),
        ],
        compiler_params=pltpu.CompilerParams(vmem_limit_bytes=58 << 20, collective_id=0, has_side_effects=True),
    )(moments, leaf_source, leaf_mask, coarse_source.T, jnp.transpose(up_shift, (0, 2, 1)), jnp.transpose(down_shift, (0, 2, 1)), far_shift)


def solution(mesh):
    cells = PartitionSpec(None, ("curve", "near"))
    copied = PartitionSpec()
    return jax.shard_map(run, mesh=mesh, in_specs=(cells,) * 4 + (copied,) * 3, out_specs=cells, check_vma=False)
```

```python
import jax, jax.numpy as jnp
from jax import lax
from jax.experimental import pallas as pl
from jax.experimental.pallas import tpu as pltpu
from jax.sharding import PartitionSpec
BF, F32, I32 = jnp.bfloat16, jnp.float32, jnp.int32
MESH = pl.DeviceIdType.MESH
P, K, C = 84, 189, 128
LO = 96
FC = 7
FW = 14


def rounded(v):
    return v.astype(BF).astype(F32)


def split(v):
    hi = v.astype(BF)
    return hi, (v - hi.astype(F32)).astype(BF)


def tail(v):
    return jnp.concatenate([v, jnp.zeros((v.shape[0], 2 * 128 - K), v.dtype)], axis=1)


def lanes(rows):
    return lax.broadcasted_iota(I32, (rows, C), 1)


def take(v, index):
    return jnp.take_along_axis(v, index, axis=1, mode="promise_in_bounds")


def kernel(m_hbm, src_hbm, msk_hbm, cs_hbm, up_hbm, dn_hbm, far_hbm, out_ref,
           win, cwin, src, msk, cs, up, dn, u3, d3, rr, z, f32, fw, fa, fb, xp, xa, xb, xc, ca, acc,
           sem, fsem, send, recv):
    nn = lax.axis_size("near")
    n = lax.axis_size("curve") * nn
    me = lax.axis_index("curve") * nn + lax.axis_index("near")
    has = (me > 0, me < n - 1)
    bar = pltpu.get_barrier_semaphore()

    def at(i):
        i = lax.rem(i + n, n)
        return (i // nn, lax.rem(i, nn))

    ends = (at(me - 1), at(me + 1))
    for side in range(2):
        @pl.when(has[side])
        def _():
            pl.semaphore_signal(bar, inc=1, device_id=ends[side], device_id_type=MESH)

    def remote(j, side):
        return pltpu.make_async_remote_copy(
            src_ref=cwin.at[1] if j else m_hbm, dst_ref=(win, cwin)[j].at[2 - 2 * side], send_sem=send.at[2 * j + side],
            recv_sem=recv.at[2 * j + 1 - side], device_id=ends[side], device_id_type=MESH)

    def each(cond, sides, act):
        for side in sides:
            @pl.when(jnp.logical_and(cond, has[side]))
            def _():
                act(side)

    def meet(cond):
        @pl.when(cond)
        def _():
            pl.semaphore_wait(bar, has[0].astype(I32) + has[1].astype(I32))

    own = pltpu.make_async_copy(m_hbm, win.at[1], sem.at[0])
    upc = pltpu.make_async_copy(up_hbm, up, sem.at[1])
    own.start()
    upc.start()
    meet(me == 0)
    each(me == 0, (0, 1), lambda side: remote(0, side).start())
    src[184:192, :] = jnp.zeros((8, C), I32)
    msk[184:192, :] = jnp.zeros((8, C), I32)
    small = [pltpu.make_async_copy(a, b, sem.at[2 + i]) for i, (a, b) in enumerate(
        ((src_hbm, src.at[0:K]), (msk_hbm, msk.at[0:K]), (cs_hbm, cs), (dn_hbm, dn)))]

    def fcopy(q):
        return pltpu.make_async_copy(far_hbm.at[:, q, :], f32.at[q], fsem.at[lax.div(q, FW)])

    def fstart(q, c):
        fcopy(q).start()
        return c

    lax.fori_loop(0, P, fstart, 0)
    for s in small:
        s.start()
    lane = lanes(P)
    rr[248:256, :] = jnp.zeros((8, C), F32)

    def triple(dst, op):
        v = op[...].reshape(8 * P, P)
        hi = rounded(v)
        dst[...] = jnp.concatenate([hi, hi, v - hi, jnp.zeros((8 * P, 4), F32)], axis=1)

    def apply(op3, x):
        hi = rounded(x)
        rr[0:P, :] = hi
        rr[P:2 * P, :] = x - hi
        rr[2 * P:3 * P, :] = hi
        z[...] = jnp.dot(op3[...], rr[...], preferred_element_type=F32)

    def pick(which):
        y = jnp.zeros((P, C), F32)
        for o in range(8):
            y = jnp.where(which == o, z[pl.ds(o, P, stride=8), :], y)
        return y

    own.wait()
    for side in range(2):
        @pl.when(jnp.logical_not(has[side]))
        def _():
            win[2 * side] = jnp.zeros((P, C), F32)
            cwin[2 * side] = jnp.zeros((P, C), F32)
    upc.wait()
    triple(u3, up)
    apply(u3, win[1])
    y = pick(lane % 8)
    for s in (1, 2, 4):
        y = y + pltpu.roll(y, C - s, 1)
    apply(u3, y)
    y = pick(jnp.where(lane % 8 == 0, (lane // 8) % 8, -1))
    for s in (8, 16, 32):
        y = y + pltpu.roll(y, C - s, 1)
    cwin[1] = y
    mid = me > 1
    meet(mid)
    each(mid, (0, 1), lambda side: (remote(0, side).start(), remote(1, side).start()))
    each(me == 0, (0, 1), lambda side: remote(1, side).start())
    for s in small:
        s.wait()

    def gather(b, steps, store, part, beside=None):
        def body(t, c):
            r = pl.ds(pl.multiple_of(t * 16, 16), 16)
            s, m = src[r, :], msk[r, :]
            index = jnp.bitwise_and(s, 127)
            hit = jnp.logical_and(lax.shift_right_logical(s, 7) == b, m > 0)
            if beside is not None:
                beside(t)
            for q in range(P):
                v = xp[q, r, :] if part else jnp.zeros((16, C), F32)
                w = jnp.broadcast_to(win[b, pl.ds(q, 1), :], (16, C))
                store(q, t, r, jnp.where(hit, take(w, index), v))
            return c
        lax.fori_loop(*steps, body, 0)

    def whole(q, t, r, v):
        xp[q, r, :] = v

    def halves_a(q, t, r, v):
        xa[q, r, 0:C], xa[q, r, C:2 * C] = split(v)

    def halves_b(q, t, r, v):
        r = pl.ds(pl.multiple_of((t - 8) * 16, 16), 16)
        xb[q, r, 0:C], xb[q, r, C:2 * C] = split(v)

    acc[...] = jnp.zeros_like(acc)
    xb[:, 64:C, :] = jnp.zeros((P, C - 64, 256), BF)
    triple(d3, dn)

    def fsplit(t):
        @pl.when(lax.rem(t, 2) == 0)
        def _():
            pltpu.make_async_copy(fw, fw, fsem.at[lax.div(t, 2)]).wait()

        for j in range(FC):
            q = t * FC + j
            l = pl.ds(pl.multiple_of(q * C, C), C)
            for f, v in ((fa, f32[q, :, 0:C]), (fb, tail(f32[q, :, C:K]))):
                f[0:P, l], f[LO:LO + P, l] = split(v)

    gather(1, (0, 12), whole, False, fsplit)
    def coarse_sources():
        w = jnp.where(lane % 64 == 0, cwin[0], jnp.where(lane % 64 == 1, pltpu.roll(cwin[1], 1, 1), pltpu.roll(cwin[2], 2, 1)))
        for m in range(2):
            for t in range(2):
                s = tail(cs[m:m + 1, 128:K]) if t else cs[m:m + 1, 0:128]
                index = jnp.bitwise_and(jnp.bitwise_and(s, 1) * 64 + lax.shift_right_logical(s, 1), 127)
                x = take(w, jnp.broadcast_to(index, (P, C)))
                for q in range(P):
                    xc[2 * m + t, q] = jnp.broadcast_to(x[q:q + 1, :], (8, C))
        ca[...] = jnp.zeros_like(ca)

    def beside_b(t):
        t = t - 8
        step = P // 4
        l = pl.ds(pl.multiple_of(t * (step * C), C), step * C)
        acc[...] += jnp.dot(fa[:, l], xa[pl.ds(t * step, step)].reshape(step * C, 2 * C), preferred_element_type=F32)
        for i in range(11):
            r = slice(8 * i, min(8 * i + 8, P))
            n = r.stop - r.start
            sums = [ca[m, r, :] for m in range(2)]
            for j in range(step):
                q = t * step + j
                u, v = f32[q, r, 0:C], tail(f32[q, r, C:K])
                for m in range(2):
                    sums[m] = sums[m] + u * xc[2 * m, q, 0:n, :] + v * xc[2 * m + 1, q, 0:n, :]
            for m in range(2):
                ca[m, r, :] = sums[m]

    one = me == 1
    right_first = jnp.logical_or(one, lax.rem(me, 2) == 0)
    rest = jnp.logical_not(right_first)
    b1 = jnp.where(right_first, 2, 0)
    each(right_first, (1,), lambda side: remote(0, 1 - side).wait_recv())
    each(rest, (0,), lambda side: remote(0, 1 - side).wait_recv())
    gather(b1, (0, 12), whole, True)
    meet(one)
    each(one, (0, 1), lambda side: (remote(0, side).start(), remote(1, side).start()))
    each(right_first, (0,), lambda side: remote(0, 1 - side).wait_recv())
    each(rest, (1,), lambda side: remote(0, 1 - side).wait_recv())
    gather(2 - b1, (0, 8), halves_a, True)
    each(True, (0, 1), lambda side: remote(1, 1 - side).wait_recv())
    coarse_sources()
    gather(2 - b1, (8, 12), halves_b, True, beside_b)
    acc[...] += jnp.dot(fb[...], xb[...].reshape(P * C, 2 * C), preferred_element_type=F32)
    cl = jnp.where(lane < 64, *(jnp.sum(ca[m], axis=1, keepdims=True) for m in range(2)))
    apply(d3, cl)
    apply(d3, pick((lane // 8) % 8))
    far = acc[0:P, 0:C] + (acc[0:P, C:2 * C] + (acc[LO:LO + P, 0:C] + acc[LO:LO + P, C:2 * C]))
    out_ref[...] = far + pick(lane % 8)
    each(True, (0, 1), lambda side: (remote(0, side).wait_send(), remote(1, side).wait_send()))


def run(moments, leaf_source, leaf_mask, coarse_source, up_shift, down_shift, far_shift):
    V = pltpu.VMEM
    D = pltpu.SemaphoreType.DMA
    return pl.pallas_call(
        kernel,
        out_shape=V((P, C), F32),
        in_specs=[pl.BlockSpec(memory_space=pl.ANY)] * 7,
        out_specs=pl.BlockSpec(memory_space=pltpu.VMEM),
        scratch_shapes=[
            V((3, P, C), F32), V((3, P, C), F32), V((192, C), I32), V((192, C), I32), V((2, K), I32),
            V((P, 8, P), F32), V((P, 8, P), F32), V((8 * P, 256), F32), V((8 * P, 256), F32), V((256, C), F32), V((8 * P, C), F32),
            V((P, P, K), F32), V((P * FW // 8, 8, K), F32), V((2 * LO, P * C), BF), V((2 * LO, P * C), BF), V((P, 192, C), F32), V((P, C, 256), BF), V((P, C, 256), BF),
            V((4, P, 8, C), F32), V((2, P, C), F32), V((2 * LO, 256), F32),
            D((6,)), D((P // FW,)), D((4,)), D((4,)),
        ],
        compiler_params=pltpu.CompilerParams(vmem_limit_bytes=58 << 20, collective_id=0, has_side_effects=True),
    )(moments, leaf_source, leaf_mask, coarse_source.T, jnp.transpose(up_shift, (0, 2, 1)), jnp.transpose(down_shift, (0, 2, 1)), far_shift)


def solution(mesh):
    cells = PartitionSpec(None, ("curve", "near"))
    copied = PartitionSpec()
    return jax.shard_map(run, mesh=mesh, in_specs=(cells,) * 4 + (copied,) * 3, out_specs=cells, check_vma=False)
```
